128 devices in a mesh: grp: 8 (over y, core), blk: 16 (over x, z).
Axes of the slice: x: 4, y: 4, z: 4, core: 2. Of those that a mesh axis runs over, the one named last changes fastest.
Arguments:
- embeddings: float32 [32768, 768], P(('grp', 'blk')), may hold values from -6 to 6
- owner: int32 [32768, 1], P(('grp', 'blk')), may hold values from 0 to 7; in each aligned block of 256 rows (0 to 255, 256 to 511, ...) at most 128 rows name the same one
- cluster: int32 [32768], P(('grp', 'blk')), may hold values from 0 to 1
- order: int32 [32768], P(('grp', 'blk')), may hold values from 0 to 32767, each once
Outputs:
- nearest: float32 [32768], P(('grp', 'blk'))
The draws below stay inside these ranges and needn't reach their ends.
Inputs may be any that keep to these rules, and one draw needn't show every extreme that they name: `owner`: in the rows of one device no group is named by more than 128 rows, a bound that some block reaches.
All inputs are finite; a program needn't handle non-finite values.
Results may differ from the reference program's by a relative error of at most 0.0013.
Values may be sent and summed in bfloat16 or wider, within the bound.
No kernel may reach another device: no remote copies, remote signals or barrier semaphores. Data moves between devices by JAX's collectives and lax.ppermute only.
A program may use at most 128 MiB of HBM per device.

```python
import math
import jax
import jax.numpy as jnp
import numpy as np
from jax import lax

D = 768
ROW_DEV = 256
CL_GRP = 2
ROWS = 32768
CAP = 128
N_GRP = 8


def set_ends(values, own_key, least, high):
    index_at = [jax.random.randint(jax.random.fold_in(own_key, axis), (), 0, length) for axis, length in enumerate(values.shape)]
    widest = values.shape.index(max(values.shape))
    beside = index_at[:widest] + [(index_at[widest] + 1) % values.shape[widest]] + index_at[widest + 1:]
    return values.at[tuple(index_at)].set(least).at[tuple(beside)].set(high)


def shard_levels(key, shape, pieces, low, top_value):
    gain, own = 1.0, jax.random.fold_in(key, 6)
    for dim, blocks in pieces:
        steps = jnp.exp(jax.random.uniform(jax.random.fold_in(own, dim), (blocks,), jnp.float32, low / len(pieces), top_value / len(pieces)))
        gain = gain * jnp.repeat(steps, shape[dim] // blocks).reshape([-1 if axis == dim else 1 for axis in range(len(shape))])
    return gain


def routed_block(own_key, own, number, rows, number_of, top, reach, slope):
    ranking = jax.random.permutation(own_key, number_of)
    heavy_load, common = shares(number_of, rows * top, reach, slope, True), shares(number_of, rows * top, reach, slope, False)
    places = jnp.arange(number_of)

    def named(sizes, rotation):
        used = int((sizes > 0).sum())
        fixed = max(1, used // 4)
        moved = fixed + (places - fixed + rotation * (used - fixed)) % max(1, number_of - fixed)
        return jnp.zeros((number_of,), jnp.int32).at[ranking[jnp.where(places < fixed, places, moved)]].set(jnp.asarray(sizes, jnp.int32))

    sizes = jnp.where(number % 4 == 0, named(heavy_load, number // 4), named(common, number - number // 4 - 1))
    mixed = jax.random.permutation(jax.random.fold_in(own, 3), number_of)
    donor, taker = mixed[0:number_of // 2 * 2:2], mixed[1:number_of // 2 * 2:2]
    slack = jnp.minimum(sizes[donor] - 1, reach - sizes[taker]) // 2
    slack = jnp.where((donor == ranking[0]) | (taker == ranking[0]) | (sizes[taker] == 0), 0, jnp.maximum(slack, 0))
    moved = jax.random.randint(jax.random.fold_in(own, 4), (number_of // 2,), 0, 1 << 20) % (slack + 1)
    sizes = sizes.at[donor].add(-moved).at[taker].add(moved)
    members = jnp.searchsorted(jnp.cumsum(sizes), jnp.arange(rows * top), side="right").astype(jnp.int32)
    table = members.reshape(top, rows).T
    table = table[jax.random.permutation(jax.random.fold_in(own, 1), rows)]
    rotation = jax.random.randint(jax.random.fold_in(own, 2), (rows, 1), 0, top)
    return jnp.take_along_axis(table, (jnp.arange(top)[None, :] + rotation) % top, axis=1)


def shares(number_of, total, bound, skew, full):
    portions = [(1 << 20) // math.isqrt(standing ** skew) + 1 for standing in range(1, number_of + 1)]
    largest = bound if full else min(bound, max(-(-total // number_of), total * portions[0] // sum(portions)))
    least = 1 if total - largest >= number_of - 1 else 0
    given, surplus = [largest] + [least] * (number_of - 1), total - largest - least * (number_of - 1)
    while surplus > 0:
        candidates = [i for i in range(1, number_of) if given[i] < largest] or [i for i in range(1, number_of) if given[i] < bound]
        mass, budget = sum([portions[i] for i in candidates]), surplus
        for i in candidates:
            extra = min(bound - given[i], max(1, budget * portions[i] // mass), surplus)
            given[i] = given[i] + extra
            surplus = surplus - extra
    return np.array(given)


def normal_values(own_key, dims, scale, bound, split=(), kind=jnp.bfloat16):
    values = jax.random.normal(own_key, dims, jnp.float32) * scale
    if len(split) > 0:
        values = shard_levels(own_key, dims, split, -0.22, 0.18) * values
    return jnp.clip(values, min=-bound, max=bound).astype(kind)


def setup_inputs(seed: int = 0) -> dict:
    streams_of = jax.random.split(jax.random.key(seed), 5)
    embeddings = normal_values(streams_of[0], (ROWS, D), 1.0, 6.0, ((0, 128),), jnp.float32)
    owner_keys = jax.random.split(jax.random.fold_in(streams_of[1], 1), ROWS // ROW_DEV)
    owner_turns = jax.random.permutation(jax.random.fold_in(streams_of[1], 3), ROWS // ROW_DEV)
    owner = jax.vmap(lambda own, number: routed_block(jax.random.fold_in(streams_of[1], 2), own, number, ROW_DEV, N_GRP, 1, CAP, 2))(owner_keys, owner_turns).reshape((ROWS, 1))
    cluster = set_ends(jax.random.randint(streams_of[2], (ROWS,), 0, CL_GRP), jax.random.fold_in(streams_of[2], 1), 0, CL_GRP - 1).astype(jnp.int32)
    order = jax.random.permutation(streams_of[3], ROWS).astype(jnp.int32)
    return {"embeddings": embeddings, "owner": owner, "cluster": cluster, "order": order}


def reference(embeddings, owner, cluster, order):
    unit = (embeddings * lax.rsqrt(lax.optimization_barrier(jnp.sum(embeddings * embeddings, axis=1, keepdims=True)) + 1e-06)).astype(jnp.bfloat16)
    ident = owner[:, 0] * CL_GRP + cluster
    block_rows = math.gcd(ROWS, 512)
    count = ROWS // block_rows

    def one_block(index):
        start = (index * block_rows).astype(jnp.int32)
        queries = lax.dynamic_slice_in_dim(unit, start, block_rows, 0)
        query_ident = lax.dynamic_slice_in_dim(ident, start, block_rows, 0)
        query_order = lax.dynamic_slice_in_dim(order, start, block_rows, 0)
        scores = lax.dot_general(queries, unit, (((1,), (1,)), ((), ())), preferred_element_type=jnp.float32)
        allowed = (query_ident[:, None] == ident[None, :]) & (order[None, :] < query_order[:, None])
        return lax.optimization_barrier(jnp.max(jnp.where(allowed, scores, jnp.float32(-1.0)), axis=1))
    nearest = lax.map(one_block, jnp.arange(count, dtype=jnp.int32))
    return nearest.reshape(ROWS)
```

```python
import functools

import jax
import jax.numpy as jnp
from jax import lax
from jax.experimental import pallas as pl
from jax.experimental.pallas import tpu as pltpu
from jax.sharding import PartitionSpec as P

GRID = 4
META = 16
SPAN = 32768.0

AXES = ("grp", "blk")


def device(x, y, z, core):
    return ((y % GRID) * 2 + core) * GRID * GRID + (x % GRID) * GRID + z % GRID


def permute(value, step):
    pairs = []
    for x in range(GRID):
        for y in range(GRID):
            for z in range(GRID):
                for core in range(2):
                    dx, dy, dz, dc = step(core)
                    pairs.append(
                        (device(x, y, z, core), device(x + dx, y + dy, z + dz, core ^ dc))
                    )
    return lax.ppermute(value, AXES, pairs)


def fetch(value, axis, sign):
    def step(core):
        offset = [0, 0, 0, 0]
        offset[axis] = -sign if core == 0 else sign
        return tuple(offset)

    return permute(value, step)


def jump(value, axis):
    def step(core):
        offset = [0, 0, 0, 0]
        offset[axis] = 2
        return tuple(offset)

    return permute(value, step)


def swap(value):
    return permute(value, lambda core: (0, 0, 0, 1))


def prepare_kernel(emb_ref, owner_ref, cluster_ref, order_ref, out_ref):
    rows, width = emb_ref.shape
    emb = emb_ref[...]
    scale = lax.rsqrt(jnp.sum(emb * emb, axis=1, keepdims=True) + 1e-06)
    out_ref[:rows, :] = (emb * scale).astype(jnp.bfloat16)
    order = order_ref[...]
    high = jnp.right_shift(order, 8)
    low = jnp.bitwise_and(order, 255)
    ident = owner_ref[...] * 2 + cluster_ref[...]
    line = lax.broadcasted_iota(jnp.int32, (META, rows), 0)
    meta = jnp.where(line == 0, high, jnp.where(line == 1, low, jnp.where(line == 2, ident, 0)))
    out_ref[rows:, :] = jnp.zeros((META, width), jnp.bfloat16)
    out_ref[rows:, :rows] = meta.astype(jnp.float32).astype(jnp.bfloat16)


def prepare(embeddings, owner, cluster, order):
    rows, width = embeddings.shape
    return pl.pallas_call(
        prepare_kernel,
        out_shape=jax.ShapeDtypeStruct((rows + META, width), jnp.bfloat16),
        compiler_params=pltpu.CompilerParams(vmem_limit_bytes=16 * 1024 * 1024),
    )(
        embeddings,
        owner.reshape(1, rows),
        cluster.reshape(1, rows),
        order.reshape(1, rows),
    )


def codes(meta):
    meta = meta.astype(jnp.float32)
    base = meta[2:3, :] * SPAN
    return base + meta[0:1, :] * 256.0 + meta[1:2, :], base


def score_kernel(counts, query_count, rows, last, *refs):
    query_refs = refs[: len(counts[0])]
    key_refs = refs[len(counts[0]) : len(counts[0]) + len(counts[1])]
    rest = refs[len(counts[0]) + len(counts[1]) :]
    place_ref, before_ref, out_ref, queries, keys, code, acc, query_sem, key_sem = rest
    block = rows + META
    copies = []
    for refs_, sizes, target, sem in (
        (query_refs, counts[0], queries, query_sem),
        (key_refs, counts[1], keys, key_sem),
    ):
        start = 0
        for index, (ref, size) in enumerate(zip(refs_, sizes)):
            copy = pltpu.make_async_copy(
                ref, target.at[pl.ds(start * block, size * block)], sem.at[index]
            )
            copy.start()
            copies.append(copy)
            start += size
    key_count = sum(counts[1])
    for copy in copies:
        copy.wait()
    acc[...] = before_ref[...]
    for index in range(query_count):
        line, _ = codes(queries[pl.ds(index * block + rows, META), :rows])
        code[index] = jnp.broadcast_to(line, (128, rows)).T

    def one_key(key_index, carry):
        key_at = pl.multiple_of(key_index * block, META)
        key = keys[pl.ds(key_at, rows), :]
        key_code, _ = codes(keys[pl.ds(key_at + rows, META), :rows])
        for index in range(query_count):
            query = queries[pl.ds(index * block, rows), :]
            scores = lax.dot_general(
                query, key, (((1,), (1,)), ((), ())), preferred_element_type=jnp.float32
            )
            query_code = code[index]
            query_base = jnp.floor(query_code * (1.0 / SPAN)) * SPAN
            best = acc[index]
            for lane in range(0, rows, 128):
                part = key_code[:, lane : lane + 128]
                allowed = (part < query_code) & (part >= query_base)
                best = jnp.maximum(best, jnp.where(allowed, scores[:, lane : lane + 128], -1.0))
            acc[index] = best
        return carry

    lax.fori_loop(0, key_count, one_key, 0)
    if last:
        for index in range(query_count):
            out_ref[place_ref[index]] = jnp.max(acc[index].T, axis=0, keepdims=True)
    else:
        out_ref[...] = acc[...]


def score(queries, keys, place, before, rows, last):
    width = queries[0].shape[1]
    block = rows + META
    sizes = [[v.shape[0] // block for v in group] for group in (queries, keys)]
    query_count, key_count = sum(sizes[0]), sum(sizes[1])
    if last:
        out = jax.ShapeDtypeStruct((query_count, 1, rows), jnp.float32)
    else:
        out = jax.ShapeDtypeStruct((query_count, rows, 128), jnp.float32)
    anywhere = pl.BlockSpec(memory_space=pl.ANY)
    vmem = pl.BlockSpec(memory_space=pltpu.VMEM)
    return pl.pallas_call(
        functools.partial(score_kernel, sizes, query_count, rows, last),
        out_shape=out,
        in_specs=[anywhere] * (len(queries) + len(keys))
        + [pl.BlockSpec(memory_space=pltpu.SMEM), vmem],
        out_specs=vmem,
        scratch_shapes=[
            pltpu.VMEM((query_count * block, width), jnp.bfloat16),
            pltpu.VMEM((key_count * block, width), jnp.bfloat16),
            pltpu.VMEM((query_count, rows, 128), jnp.float32),
            pltpu.VMEM((query_count, rows, 128), jnp.float32),
            pltpu.SemaphoreType.DMA((len(queries),)),
            pltpu.SemaphoreType.DMA((len(keys),)),
        ],
        compiler_params=pltpu.CompilerParams(vmem_limit_bytes=32 * 1024 * 1024),
        cost_estimate=pl.CostEstimate(
            flops=2 * query_count * key_count * rows * rows * width,
            bytes_accessed=(query_count + key_count) * block * width * 2,
            transcendentals=0,
        ),
    )(*queries, *keys, place, before)


def local(embeddings, owner, cluster, order):
    rows = embeddings.shape[0]
    block = rows + META
    own = prepare(embeddings, owner, cluster, order)
    pair = jnp.concatenate([own, swap(own)], axis=0)
    key_x = fetch(pair, 0, 1)
    key_z = fetch(pair, 2, 1)
    line_y = fetch(pair, 1, 1)
    far_y = jump(own, 1)
    key_xz = fetch(key_x, 2, -1)
    key_zz = fetch(key_z[:block], 2, 1)
    key_xx = fetch(jnp.concatenate([key_x[:block], key_z], axis=0), 0, 1)
    other_y = swap(jnp.concatenate([line_y, far_y], axis=0))
    key_xzz = fetch(key_xz, 2, -1)
    key_xxz = fetch(key_xz, 0, 1)
    key_far = jump(key_zz, 0)
    queries = [pair, line_y, far_y, other_y]
    index = lax.axis_index("grp")
    y, core = index // 2, index % 2
    side = 1 - 2 * core
    where_y = jnp.stack([y, y, y + side, y + side, y + 2, y - side, y - side, y + 2]) % GRID
    types = jnp.stack([core, 1 - core, core, 1 - core, core, 1 - core, core, 1 - core])
    place = (where_y * 2 + types).astype(jnp.int32)
    best = jnp.full((8, rows, 128), -1.0, jnp.float32)
    best = score(queries, [own, key_x, key_z], place, best, rows, False)
    best = score(queries, [key_xz, key_zz, key_xx], place, best, rows, False)
    best = score(queries, [key_xzz, key_xxz], place, best, rows, False)
    best = score(queries, [key_far], place, best, rows, True)
    home = lax.all_to_all(best, "grp", split_axis=0, concat_axis=0, tiled=True)
    return jnp.max(home.reshape(8, rows), axis=0)


def solution(mesh):
    placed = (
        P(("grp", "blk"), None),
        P(("grp", "blk"), None),
        P(("grp", "blk")),
        P(("grp", "blk")),
    )
    return jax.shard_map(
        local, mesh=mesh, in_specs=placed, out_specs=P(("grp", "blk")), check_vma=False
    )
```

```python
import functools

import jax
import jax.numpy as jnp
from jax import lax
from jax.experimental import pallas as pl
from jax.experimental.pallas import tpu as pltpu
from jax.sharding import PartitionSpec as P

GRID = 4
META = 16
SPAN = 32768.0

AXES = ("grp", "blk")


def device(x, y, z, core):
    return ((y % GRID) * 2 + core) * GRID * GRID + (x % GRID) * GRID + z % GRID


def permute(value, step):
    pairs = []
    for x in range(GRID):
        for y in range(GRID):
            for z in range(GRID):
                for core in range(2):
                    dx, dy, dz, dc = step(core)
                    pairs.append(
                        (device(x, y, z, core), device(x + dx, y + dy, z + dz, core ^ dc))
                    )
    return lax.ppermute(value, AXES, pairs)


def fetch(value, axis, sign):
    def step(core):
        offset = [0, 0, 0, 0]
        offset[axis] = -sign if core == 0 else sign
        return tuple(offset)

    return permute(value, step)


def jump(value, axis):
    def step(core):
        offset = [0, 0, 0, 0]
        offset[axis] = 2
        return tuple(offset)

    return permute(value, step)


def swap(value):
    return permute(value, lambda core: (0, 0, 0, 1))


def prepare_kernel(emb_ref, numbers_ref, out_ref):
    rows, width = emb_ref.shape
    owner, cluster, order = numbers_ref[0:1, :], numbers_ref[1:2, :], numbers_ref[2:3, :]
    high = jnp.right_shift(order, 8)
    low = jnp.bitwise_and(order, 255)
    ident = owner * 2 + cluster
    line = lax.broadcasted_iota(jnp.int32, (META, rows), 0)
    meta = jnp.where(line == 0, high, jnp.where(line == 1, low, jnp.where(line == 2, ident, 0)))
    out_ref[rows:, :] = jnp.zeros((META, width), jnp.bfloat16)
    out_ref[rows:, :rows] = meta.astype(jnp.float32).astype(jnp.bfloat16)
    values = emb_ref[...]
    scale = lax.rsqrt(jnp.sum(values * values, axis=1, keepdims=True) + 1e-06)
    out_ref[:rows, :] = (values * scale).astype(jnp.bfloat16)


def prepare(embeddings, owner, cluster, order):
    rows, width = embeddings.shape
    vmem = pl.BlockSpec(memory_space=pltpu.VMEM)
    numbers = jnp.concatenate(
        [owner.reshape(1, rows), cluster.reshape(1, rows), order.reshape(1, rows)], axis=0
    )
    return pl.pallas_call(
        prepare_kernel,
        out_shape=jax.ShapeDtypeStruct((rows + META, width), jnp.bfloat16),
        in_specs=[vmem] * 2,
        out_specs=vmem,
        compiler_params=pltpu.CompilerParams(vmem_limit_bytes=16 * 1024 * 1024),
    )(embeddings, numbers)


def codes(meta):
    meta = meta.astype(jnp.float32)
    base = meta[2:3, :] * SPAN
    return base + meta[0:1, :] * 256.0 + meta[1:2, :], base


def score_kernel(tasks, sizes, columns_of, rows, last, *refs):
    block = rows + META
    refs = list(refs)
    arrays = [refs.pop(0) for _ in sizes]
    befores = [refs.pop(0) if more else None for _, _, more in tasks]
    place = refs.pop(0) if last else None
    columns = refs.pop()
    for name, slot in columns_of.items():
        for index in range(sizes[name]):
            line, _ = codes(arrays[name][index * block + rows : (index + 1) * block, :rows])
            columns[slot + index] = jnp.broadcast_to(line, (128, rows)).T
    done = 0
    for number, (queries, keys, _) in enumerate(tasks):
        places = [(name, index) for name in queries for index in range(sizes[name])]
        for query, (query_name, query_index) in enumerate(places):
            at = query_index * block
            code, base = codes(arrays[query_name][at + rows : at + block, :rows])
            before = befores[number]
            most = jnp.full((8, rows), -1.0, jnp.float32) if before is None else before[query]
            for name in keys:
                for index in range(sizes[name]):
                    scores = lax.dot_general(
                        arrays[name][index * block : index * block + rows, :],
                        arrays[query_name][at : at + rows, :],
                        (((1,), (1,)), ((), ())),
                        preferred_element_type=jnp.float32,
                    )
                    column = columns[columns_of[name] + index]
                    column = jnp.concatenate([column] * (rows // 128), axis=1)
                    allowed = (column < code) & (column >= base)
                    scores = jnp.where(allowed, scores, -1.0).reshape(rows // 8, 8, rows)
                    most = jnp.maximum(most, scores.max(axis=0))
            if last:
                refs[0][place[done]] = jnp.max(most, axis=0, keepdims=True)
            else:
                refs[number][query] = most
            done += 1


def score(tasks, rows, place=None):
    block = rows + META
    arrays = []

    def position(value):
        for index, other in enumerate(arrays):
            if other is value:
                return index
        arrays.append(value)
        return len(arrays) - 1

    plan = tuple(
        (tuple(map(position, queries)), tuple(map(position, keys)), before is not None)
        for queries, keys, before in tasks
    )
    width = arrays[0].shape[1]
    sizes = tuple(v.shape[0] // block for v in arrays)
    columns_of, count = {}, 0
    for _, keys, _ in plan:
        for name in keys:
            if name not in columns_of:
                columns_of[name] = count
                count += sizes[name]
    query_counts = [sum(sizes[n] for n in queries) for queries, _, _ in plan]
    pairs = sum(
        total * sum(sizes[n] for n in keys) for total, (_, keys, _) in zip(query_counts, plan)
    )
    befores = [before for _, _, before in tasks if before is not None]
    last = place is not None
    if last:
        out_shape = [jax.ShapeDtypeStruct((sum(query_counts), 1, rows), jnp.float32)]
    else:
        out_shape = [jax.ShapeDtypeStruct((total, 8, rows), jnp.float32) for total in query_counts]
    vmem = pl.BlockSpec(memory_space=pltpu.VMEM)
    return pl.pallas_call(
        functools.partial(score_kernel, plan, sizes, columns_of, rows, last),
        out_shape=out_shape,
        in_specs=[vmem] * (len(arrays) + len(befores))
        + [pl.BlockSpec(memory_space=pltpu.SMEM)] * last,
        out_specs=[vmem] * len(out_shape),
        scratch_shapes=[pltpu.VMEM((count, rows, 128), jnp.float32)],
        compiler_params=pltpu.CompilerParams(vmem_limit_bytes=8 * 1024 * 1024),
        cost_estimate=pl.CostEstimate(
            flops=2 * pairs * rows * width, bytes_accessed=10000, transcendentals=0
        ),
    )(*arrays, *befores, *([place] if last else []))


def local(embeddings, owner, cluster, order):
    rows = embeddings.shape[0]
    block = rows + META
    index = lax.axis_index("grp")
    y, core = index // 2, index % 2
    side = 1 - 2 * core
    steps = jnp.stack([y, y, y + side, y + side, y - side, y - side, y + 2, y + 2]) % GRID
    types = jnp.stack([core, 1 - core, core, 1 - core, 1 - core, core, core, 1 - core])
    place = (steps * 2 + types).astype(jnp.int32)
    own = prepare(embeddings, owner, cluster, order)
    pair = jnp.concatenate([own, swap(own)], axis=0)
    key_x = fetch(pair, 0, 1)
    key_z = fetch(pair, 2, 1)
    line_y = fetch(pair, 1, 1)
    line_2y = fetch(line_y, 1, 1)
    key_xz = fetch(key_x, 2, -1)
    key_zx = fetch(jnp.concatenate([key_x[:block], key_z], axis=0), 0, 1)
    key_2z = fetch(key_z[:block], 2, 1)
    other_y = swap(line_y)
    front, back = [pair, line_y], [other_y, line_2y]
    near = [own, key_x, key_z]
    (best_front,) = score([(front, near, None)], rows)
    key_xz, best_front = lax.optimization_barrier((key_xz, best_front))
    key_2x2z = jump(key_2z, 0)
    key_xzz = fetch(key_xz, 2, -1)
    key_xxz = fetch(key_xz, 0, 1)
    middle = [key_xz, key_zx, key_2z]
    best_front, best_back = score(
        [(front, middle, best_front), (back, near + middle, None)], rows
    )
    far = [key_xxz, key_xzz, key_2x2z]
    (best,) = score([(front, far, best_front), (back, far, best_back)], rows, place)
    home = lax.all_to_all(best, "grp", split_axis=0, concat_axis=0, tiled=True)
    return jnp.max(home.reshape(8, rows), axis=0)


def solution(mesh):
    placed = (
        P(("grp", "blk"), None),
        P(("grp", "blk"), None),
        P(("grp", "blk")),
        P(("grp", "blk")),
    )
    return jax.shard_map(
        local, mesh=mesh, in_specs=placed, out_specs=P(("grp", "blk")), check_vma=False
    )
```

```python
import functools

import jax
import jax.numpy as jnp
from jax import lax
from jax.experimental import pallas as pl
from jax.experimental.pallas import tpu as pltpu
from jax.sharding import PartitionSpec as P

GRID = 4
META = 16
SPAN = 32768.0

AXES = ("grp", "blk")


def device(x, y, z, core):
    return ((y % GRID) * 2 + core) * GRID * GRID + (x % GRID) * GRID + z % GRID


def permute(value, step):
    pairs = []
    for x in range(GRID):
        for y in range(GRID):
            for z in range(GRID):
                for core in range(2):
                    dx, dy, dz, dc = step(core)
                    pairs.append(
                        (device(x, y, z, core), device(x + dx, y + dy, z + dz, core ^ dc))
                    )
    return lax.ppermute(value, AXES, pairs)


def fetch(value, axis, sign):
    def step(core):
        offset = [0, 0, 0, 0]
        offset[axis] = -sign if core == 0 else sign
        return tuple(offset)

    return permute(value, step)


def jump(value, axis):
    def step(core):
        offset = [0, 0, 0, 0]
        offset[axis] = 2
        return tuple(offset)

    return permute(value, step)


def swap(value):
    return permute(value, lambda core: (0, 0, 0, 1))


def prepare_kernel(emb_ref, numbers_ref, out_ref):
    rows, width = emb_ref.shape
    owner, cluster, order = numbers_ref[0:1, :], numbers_ref[1:2, :], numbers_ref[2:3, :]
    high = jnp.right_shift(order, 8)
    low = jnp.bitwise_and(order, 255)
    ident = owner * 2 + cluster
    line = lax.broadcasted_iota(jnp.int32, (META, rows), 0)
    meta = jnp.where(line == 0, high, jnp.where(line == 1, low, jnp.where(line == 2, ident, 0)))
    out_ref[rows:, :] = jnp.zeros((META, width), jnp.bfloat16)
    out_ref[rows:, :rows] = meta.astype(jnp.float32).astype(jnp.bfloat16)
    values = emb_ref[...]
    scale = lax.rsqrt(jnp.sum(values * values, axis=1, keepdims=True) + 1e-06)
    out_ref[:rows, :] = (values * scale).astype(jnp.bfloat16)


def prepare(embeddings, owner, cluster, order):
    rows, width = embeddings.shape
    vmem = pl.BlockSpec(memory_space=pltpu.VMEM)
    numbers = jnp.concatenate(
        [owner.reshape(1, rows), cluster.reshape(1, rows), order.reshape(1, rows)], axis=0
    )
    return pl.pallas_call(
        prepare_kernel,
        out_shape=jax.ShapeDtypeStruct((rows + META, width), jnp.bfloat16),
        in_specs=[vmem] * 2,
        out_specs=vmem,
        compiler_params=pltpu.CompilerParams(vmem_limit_bytes=8 * 1024 * 1024),
    )(embeddings, numbers)


def codes(meta):
    meta = meta.astype(jnp.float32)
    base = meta[2:3, :] * SPAN
    return base + meta[0:1, :] * 256.0 + meta[1:2, :], base


def score_kernel(tasks, sizes, columns_of, rows, last, *refs):
    block = rows + META
    refs = list(refs)
    arrays = [refs.pop(0) for _ in sizes]
    befores = [refs.pop(0) if more else None for _, _, more in tasks]
    place = refs.pop(0) if last else None
    columns = refs.pop()
    made = set()

    def column_of(name, index):
        if (name, index) not in made:
            made.add((name, index))
            line, _ = codes(arrays[name][index * block + rows : (index + 1) * block, :rows])
            columns[columns_of[name] + index] = jnp.broadcast_to(line, (128, rows)).T
        return columns[columns_of[name] + index]

    done = 0
    for number, (queries, keys, _) in enumerate(tasks):
        places = [(name, index) for name in queries for index in range(sizes[name])]
        for query, (query_name, query_index) in enumerate(places):
            at = query_index * block
            code, base = codes(arrays[query_name][at + rows : at + block, :rows])
            before = befores[number]
            most = jnp.full((8, rows), -1.0, jnp.float32) if before is None else before[query]
            for name in keys:
                for index in range(sizes[name]):
                    scores = lax.dot_general(
                        arrays[name][index * block : index * block + rows, :],
                        arrays[query_name][at : at + rows, :],
                        (((1,), (1,)), ((), ())),
                        preferred_element_type=jnp.float32,
                    )
                    column = column_of(name, index)
                    column = jnp.concatenate([column] * (rows // 128), axis=1)
                    allowed = (column < code) & (column >= base)
                    scores = jnp.where(allowed, scores, -1.0).reshape(rows // 8, 8, rows)
                    most = jnp.maximum(most, scores.max(axis=0))
            if last:
                refs[0][place[done]] = jnp.max(most, axis=0, keepdims=True)
            else:
                refs[number][query] = most
            done += 1


def score(tasks, rows, place=None):
    block = rows + META
    arrays = []

    def position(value):
        for index, other in enumerate(arrays):
            if other is value:
                return index
        arrays.append(value)
        return len(arrays) - 1

    plan = tuple(
        (tuple(map(position, queries)), tuple(map(position, keys)), before is not None)
        for queries, keys, before in tasks
    )
    width = arrays[0].shape[1]
    sizes = tuple(v.shape[0] // block for v in arrays)
    columns_of, count = {}, 0
    for _, keys, _ in plan:
        for name in keys:
            if name not in columns_of:
                columns_of[name] = count
                count += sizes[name]
    query_counts = [sum(sizes[n] for n in queries) for queries, _, _ in plan]
    pairs = sum(
        total * sum(sizes[n] for n in keys) for total, (_, keys, _) in zip(query_counts, plan)
    )
    befores = [before for _, _, before in tasks if before is not None]
    last = place is not None
    if last:
        out_shape = [jax.ShapeDtypeStruct((sum(query_counts), 1, rows), jnp.float32)]
    else:
        out_shape = [jax.ShapeDtypeStruct((total, 8, rows), jnp.float32) for total in query_counts]
    vmem = pl.BlockSpec(memory_space=pltpu.VMEM)
    return pl.pallas_call(
        functools.partial(score_kernel, plan, sizes, columns_of, rows, last),
        out_shape=out_shape,
        in_specs=[vmem] * (len(arrays) + len(befores))
        + [pl.BlockSpec(memory_space=pltpu.SMEM)] * last,
        out_specs=[vmem] * len(out_shape),
        scratch_shapes=[pltpu.VMEM((count, rows, 128), jnp.float32)],
        compiler_params=pltpu.CompilerParams(vmem_limit_bytes=4 * 1024 * 1024),
        cost_estimate=pl.CostEstimate(
            flops=2 * pairs * rows * width, bytes_accessed=10000, transcendentals=0
        ),
    )(*arrays, *befores, *([place] if last else []))


def pick_kernel(parts, block, *refs):
    out = refs[-1]
    for at, (name, index) in enumerate(parts):
        out[at * block : (at + 1) * block, :] = refs[name][index * block : (index + 1) * block, :]


def pick(parts, rows):
    block = rows + META
    arrays, plan = [], []
    for value, index in parts:
        known = [at for at, other in enumerate(arrays) if other is value]
        if not known:
            arrays.append(value)
        plan.append((known[0] if known else len(arrays) - 1, index))
    vmem = pl.BlockSpec(memory_space=pltpu.VMEM)
    return pl.pallas_call(
        functools.partial(pick_kernel, tuple(plan), block),
        out_shape=jax.ShapeDtypeStruct((len(parts) * block, arrays[0].shape[1]), arrays[0].dtype),
        in_specs=[vmem] * len(arrays),
        out_specs=vmem,
        compiler_params=pltpu.CompilerParams(vmem_limit_bytes=4 * 1024 * 1024),
        cost_estimate=pl.CostEstimate(flops=0, bytes_accessed=10000, transcendentals=0),
    )(*arrays)


def local(embeddings, owner, cluster, order):
    rows = embeddings.shape[0]
    index = lax.axis_index("grp")
    y, core = index // 2, index % 2
    side = 1 - 2 * core
    steps = jnp.stack([y, y, y + side, y + side, y - side, y - side, y + 2, y + 2]) % GRID
    types = jnp.stack([core, 1 - core, core, 1 - core, 1 - core, core, core, 1 - core])
    place = (steps * 2 + types).astype(jnp.int32)
    own = prepare(embeddings, owner, cluster, order)
    sib = swap(own)
    sib, place = lax.optimization_barrier((sib, place))
    pair = pick([(own, 0), (sib, 0)], rows)
    key_x = fetch(pair, 0, 1)
    key_z = fetch(pair, 2, 1)
    line_y = fetch(pair, 1, 1)
    line_2y = fetch(line_y, 1, 1)
    key_xz = fetch(key_x, 2, -1)
    key_zx = fetch(pick([(key_x, 0), (key_z, 0), (key_z, 1)], rows), 0, 1)
    other_y = swap(line_y)
    front, back = [pair, line_y, other_y], [line_2y]
    near = [own, key_x, key_z]
    (best_front,) = score([(front, near, None)], rows)
    key_2z = fetch(pick([(key_z, 0)], rows), 2, 1)
    key_xz, best_front = lax.optimization_barrier((key_xz, best_front))
    key_2x2z = jump(key_2z, 0)
    key_xzz = fetch(key_xz, 2, -1)
    key_xxz = fetch(pick([(key_xz, 0)], rows), 0, 1)
    far = [key_xxz, key_xzz, fetch(pick([(key_zx, 0)], rows), 2, 1), key_2x2z]
    middle = [key_xz, key_zx, key_2z]
    best_front, best_back = score(
        [(front, middle, best_front), (back, near + middle, None)], rows
    )
    (best,) = score([(front, far, best_front), (back, far, best_back)], rows, place)
    home = lax.all_to_all(best, "grp", split_axis=0, concat_axis=0, tiled=True)
    return jnp.max(home.reshape(8, rows), axis=0)


def solution(mesh):
    placed = (
        P(("grp", "blk"), None),
        P(("grp", "blk"), None),
        P(("grp", "blk")),
        P(("grp", "blk")),
    )
    return jax.shard_map(
        local, mesh=mesh, in_specs=placed, out_specs=P(("grp", "blk")), check_vma=False
    )
```

```python
import functools

import jax
import jax.numpy as jnp
from jax import lax
from jax.experimental import pallas as pl
from jax.experimental.pallas import tpu as pltpu
from jax.sharding import PartitionSpec as P

GRID = 4
META = 16
SPAN = 32768.0

AXES = ("grp", "blk")


def device(x, y, z, core):
    return ((y % GRID) * 2 + core) * GRID * GRID + (x % GRID) * GRID + z % GRID


def permute(value, step):
    pairs = []
    for x in range(GRID):
        for y in range(GRID):
            for z in range(GRID):
                for core in range(2):
                    dx, dy, dz, dc = step(core)
                    pairs.append(
                        (device(x, y, z, core), device(x + dx, y + dy, z + dz, core ^ dc))
                    )
    return lax.ppermute(value, AXES, pairs)


def fetch(value, axis, sign):
    def step(core):
        offset = [0, 0, 0, 0]
        offset[axis] = -sign if core == 0 else sign
        return tuple(offset)

    return permute(value, step)


def jump(value, axis):
    def step(core):
        offset = [0, 0, 0, 0]
        offset[axis] = 2
        return tuple(offset)

    return permute(value, step)


def swap(value):
    return permute(value, lambda core: (0, 0, 0, 1))


def write_block(emb_ref, numbers_ref, out_ref, start):
    rows, width = emb_ref.shape
    owner, cluster, order = numbers_ref[0:1, :], numbers_ref[1:2, :], numbers_ref[2:3, :]
    high = jnp.right_shift(order, 8)
    low = jnp.bitwise_and(order, 255)
    ident = owner * 2 + cluster
    line = lax.broadcasted_iota(jnp.int32, (META, rows), 0)
    meta = jnp.where(line == 0, high, jnp.where(line == 1, low, jnp.where(line == 2, ident, 0)))
    end = start + rows
    out_ref[end : end + META, :] = jnp.zeros((META, width), jnp.bfloat16)
    out_ref[end : end + META, :rows] = meta.astype(jnp.float32).astype(jnp.bfloat16)
    values = emb_ref[...]
    scale = lax.rsqrt(jnp.sum(values * values, axis=1, keepdims=True) + 1e-06)
    out_ref[start:end, :] = (values * scale).astype(jnp.bfloat16)


def own_kernel(emb_ref, numbers_ref, out_ref):
    write_block(emb_ref, numbers_ref, out_ref, 0)


def pair_kernel(own_ref, emb_ref, numbers_ref, out_ref):
    block = own_ref.shape[0]
    out_ref[:block, :] = own_ref[...]
    write_block(emb_ref, numbers_ref, out_ref, block)


def prepare(embeddings, owner, cluster, order):
    rows, width = embeddings.shape
    vmem = pl.BlockSpec(memory_space=pltpu.VMEM)
    numbers = jnp.concatenate(
        [owner.reshape(1, rows), cluster.reshape(1, rows), order.reshape(1, rows)], axis=0
    )
    other, other_numbers = swap(embeddings), swap(numbers)
    params = pltpu.CompilerParams(vmem_limit_bytes=8 * 1024 * 1024)
    own = pl.pallas_call(
        own_kernel,
        out_shape=jax.ShapeDtypeStruct((rows + META, width), jnp.bfloat16),
        in_specs=[vmem] * 2,
        out_specs=vmem,
        compiler_params=params,
        cost_estimate=pl.CostEstimate(flops=0, bytes_accessed=10000, transcendentals=0),
    )(embeddings, numbers)
    pair = pl.pallas_call(
        pair_kernel,
        out_shape=jax.ShapeDtypeStruct((2 * (rows + META), width), jnp.bfloat16),
        in_specs=[vmem] * 3,
        out_specs=vmem,
        compiler_params=params,
        cost_estimate=pl.CostEstimate(flops=0, bytes_accessed=10000, transcendentals=0),
    )(own, other, other_numbers)
    return own, pair


def codes(meta):
    meta = meta.astype(jnp.float32)
    base = meta[2:3, :] * SPAN
    return base + meta[0:1, :] * 256.0 + meta[1:2, :], base


def score_kernel(tasks, sizes, columns_of, rows, last, *refs):
    block = rows + META
    refs = list(refs)
    arrays = [refs.pop(0) for _ in sizes]
    befores = [refs.pop(0) if more else None for _, _, more in tasks]
    place = refs.pop(0) if last else None
    columns = refs.pop()
    made = set()

    def column_of(name, index):
        if (name, index) not in made:
            made.add((name, index))
            line, _ = codes(arrays[name][index * block + rows : (index + 1) * block, :rows])
            columns[columns_of[name] + index] = jnp.broadcast_to(line, (128, rows)).T
        return columns[columns_of[name] + index]

    done = 0
    for number, (queries, keys, _) in enumerate(tasks):
        places = [(name, index) for name in queries for index in range(sizes[name])]
        for query, (query_name, query_index) in enumerate(places):
            at = query_index * block
            code, base = codes(arrays[query_name][at + rows : at + block, :rows])
            before = befores[number]
            most = jnp.full((8, rows), -1.0, jnp.float32) if before is None else before[query]
            for name in keys:
                for index in range(sizes[name]):
                    scores = lax.dot_general(
                        arrays[name][index * block : index * block + rows, :],
                        arrays[query_name][at : at + rows, :],
                        (((1,), (1,)), ((), ())),
                        preferred_element_type=jnp.float32,
                    )
                    column = column_of(name, index)
                    column = jnp.concatenate([column] * (rows // 128), axis=1)
                    allowed = (column < code) & (column >= base)
                    scores = jnp.where(allowed, scores, -1.0).reshape(rows // 8, 8, rows)
                    most = jnp.maximum(most, scores.max(axis=0))
            if last:
                refs[0][place[done]] = jnp.max(most, axis=0, keepdims=True)
            else:
                refs[number][query] = most
            done += 1


def score(tasks, rows, place=None):
    block = rows + META
    arrays = []

    def position(value):
        for index, other in enumerate(arrays):
            if other is value:
                return index
        arrays.append(value)
        return len(arrays) - 1

    plan = tuple(
        (tuple(map(position, queries)), tuple(map(position, keys)), before is not None)
        for queries, keys, before in tasks
    )
    width = arrays[0].shape[1]
    sizes = tuple(v.shape[0] // block for v in arrays)
    columns_of, count = {}, 0
    for _, keys, _ in plan:
        for name in keys:
            if name not in columns_of:
                columns_of[name] = count
                count += sizes[name]
    query_counts = [sum(sizes[n] for n in queries) for queries, _, _ in plan]
    pairs = sum(
        total * sum(sizes[n] for n in keys) for total, (_, keys, _) in zip(query_counts, plan)
    )
    befores = [before for _, _, before in tasks if before is not None]
    last = place is not None
    if last:
        out_shape = [jax.ShapeDtypeStruct((sum(query_counts), 1, rows), jnp.float32)]
    else:
        out_shape = [jax.ShapeDtypeStruct((total, 8, rows), jnp.float32) for total in query_counts]
    vmem = pl.BlockSpec(memory_space=pltpu.VMEM)
    return pl.pallas_call(
        functools.partial(score_kernel, plan, sizes, columns_of, rows, last),
        out_shape=out_shape,
        in_specs=[vmem] * (len(arrays) + len(befores))
        + [pl.BlockSpec(memory_space=pltpu.SMEM)] * last,
        out_specs=[vmem] * len(out_shape),
        scratch_shapes=[pltpu.VMEM((count, rows, 128), jnp.float32)],
        compiler_params=pltpu.CompilerParams(vmem_limit_bytes=4 * 1024 * 1024),
        cost_estimate=pl.CostEstimate(
            flops=2 * pairs * rows * width, bytes_accessed=10000, transcendentals=0
        ),
    )(*arrays, *befores, *([place] if last else []))


def pick_kernel(parts, block, *refs):
    out = refs[-1]
    for at, (name, index) in enumerate(parts):
        out[at * block : (at + 1) * block, :] = refs[name][index * block : (index + 1) * block, :]


def pick(parts, rows):
    block = rows + META
    arrays, plan = [], []
    for value, index in parts:
        known = [at for at, other in enumerate(arrays) if other is value]
        if not known:
            arrays.append(value)
        plan.append((known[0] if known else len(arrays) - 1, index))
    vmem = pl.BlockSpec(memory_space=pltpu.VMEM)
    return pl.pallas_call(
        functools.partial(pick_kernel, tuple(plan), block),
        out_shape=jax.ShapeDtypeStruct((len(parts) * block, arrays[0].shape[1]), arrays[0].dtype),
        in_specs=[vmem] * len(arrays),
        out_specs=vmem,
        compiler_params=pltpu.CompilerParams(vmem_limit_bytes=4 * 1024 * 1024),
        cost_estimate=pl.CostEstimate(flops=0, bytes_accessed=10000, transcendentals=0),
    )(*arrays)


def local(embeddings, owner, cluster, order):
    rows = embeddings.shape[0]
    index = lax.axis_index("grp")
    y, core = index // 2, index % 2
    side = 1 - 2 * core
    steps = jnp.stack([y, y, y + side, y + side, y - side, y - side, y + 2, y + 2]) % GRID
    types = jnp.stack([core, 1 - core, core, 1 - core, 1 - core, core, core, 1 - core])
    place = (steps * 2 + types).astype(jnp.int32)
    own, pair = prepare(embeddings, owner, cluster, order)
    pair, place = lax.optimization_barrier((pair, place))
    key_x = fetch(pair, 0, 1)
    key_z = fetch(pair, 2, 1)
    line_y = fetch(pair, 1, 1)
    line_2y = fetch(line_y, 1, 1)
    key_xz = fetch(key_x, 2, -1)
    key_zx = fetch(pick([(key_x, 0), (key_z, 0), (key_z, 1)], rows), 0, 1)
    other_y = swap(line_y)
    front, back = [pair, line_y, other_y], [line_2y]
    near = [own, key_x, key_z]
    (best_front,) = score([(front, near, None)], rows)
    key_2z = fetch(pick([(key_z, 0)], rows), 2, 1)
    key_xz, best_front = lax.optimization_barrier((key_xz, best_front))
    key_2x2z = jump(key_2z, 0)
    key_xzz = fetch(key_xz, 2, -1)
    key_xxz = fetch(pick([(key_xz, 0)], rows), 0, 1)
    far = [key_xxz, key_xzz, fetch(pick([(key_zx, 0)], rows), 2, 1), key_2x2z]
    middle = [key_xz, key_zx, key_2z]
    best_front, best_back = score(
        [(front, middle, best_front), (back, near + middle, None)], rows
    )
    (best,) = score([(front, far, best_front), (back, far, best_back)], rows, place)
    home = lax.all_to_all(best, "grp", split_axis=0, concat_axis=0, tiled=True)
    return jnp.max(home.reshape(8, rows), axis=0)


def solution(mesh):
    placed = (
        P(("grp", "blk"), None),
        P(("grp", "blk"), None),
        P(("grp", "blk")),
        P(("grp", "blk")),
    )
    return jax.shard_map(
        local, mesh=mesh, in_specs=placed, out_specs=P(("grp", "blk")), check_vma=False
    )
```

```python
import functools

import jax
import jax.numpy as jnp
from jax import lax
from jax.experimental import pallas as pl
from jax.experimental.pallas import tpu as pltpu
from jax.sharding import PartitionSpec as P

GRID = 4
META = 16
SPAN = 32768.0

AXES = ("grp", "blk")


def device(x, y, z, core):
    return ((y % GRID) * 2 + core) * GRID * GRID + (x % GRID) * GRID + z % GRID


def permute(value, step):
    pairs = []
    for x in range(GRID):
        for y in range(GRID):
            for z in range(GRID):
                for core in range(2):
                    dx, dy, dz, dc = step(core)
                    pairs.append(
                        (device(x, y, z, core), device(x + dx, y + dy, z + dz, core ^ dc))
                    )
    return lax.ppermute(value, AXES, pairs)


def fetch(value, axis, sign):
    def step(core):
        offset = [0, 0, 0, 0]
        offset[axis] = -sign if core == 0 else sign
        return tuple(offset)

    return permute(value, step)


def jump(value, axis):
    def step(core):
        offset = [0, 0, 0, 0]
        offset[axis] = 2
        return tuple(offset)

    return permute(value, step)


def swap(value):
    return permute(value, lambda core: (0, 0, 0, 1))


def write_block(emb_ref, numbers_ref, out_ref, start):
    rows, width = emb_ref.shape
    owner, cluster, order = numbers_ref[0:1, :], numbers_ref[1:2, :], numbers_ref[2:3, :]
    high = jnp.right_shift(order, 8)
    low = jnp.bitwise_and(order, 255)
    ident = owner * 2 + cluster
    line = lax.broadcasted_iota(jnp.int32, (META, rows), 0)
    meta = jnp.where(line == 0, high, jnp.where(line == 1, low, jnp.where(line == 2, ident, 0)))
    end = start + rows
    out_ref[end : end + META, :] = jnp.zeros((META, width), jnp.bfloat16)
    out_ref[end : end + META, :rows] = meta.astype(jnp.float32).astype(jnp.bfloat16)
    values = emb_ref[...]
    scale = lax.rsqrt(jnp.sum(values * values, axis=1, keepdims=True) + 1e-06)
    out_ref[start:end, :] = (values * scale).astype(jnp.bfloat16)


def own_kernel(emb_ref, numbers_ref, out_ref):
    write_block(emb_ref, numbers_ref, out_ref, 0)


def pair_kernel(own_ref, emb_ref, numbers_ref, out_ref):
    block = own_ref.shape[0]
    out_ref[:block, :] = own_ref[...]
    write_block(emb_ref, numbers_ref, out_ref, block)


def prepare(embeddings, owner, cluster, order):
    rows, width = embeddings.shape
    vmem = pl.BlockSpec(memory_space=pltpu.VMEM)
    numbers = jnp.concatenate(
        [owner.reshape(1, rows), cluster.reshape(1, rows), order.reshape(1, rows)], axis=0
    )
    other, other_numbers = swap(embeddings), swap(numbers)
    params = pltpu.CompilerParams(vmem_limit_bytes=8 * 1024 * 1024)
    own = pl.pallas_call(
        own_kernel,
        out_shape=jax.ShapeDtypeStruct((rows + META, width), jnp.bfloat16),
        in_specs=[vmem] * 2,
        out_specs=vmem,
        compiler_params=params,
        cost_estimate=pl.CostEstimate(flops=0, bytes_accessed=10000, transcendentals=0),
    )(embeddings, numbers)
    pair = pl.pallas_call(
        pair_kernel,
        out_shape=jax.ShapeDtypeStruct((2 * (rows + META), width), jnp.bfloat16),
        in_specs=[vmem] * 3,
        out_specs=vmem,
        compiler_params=params,
        cost_estimate=pl.CostEstimate(flops=0, bytes_accessed=10000, transcendentals=0),
    )(own, other, other_numbers)
    return own, pair


def codes(meta):
    meta = meta.astype(jnp.float32)
    base = meta[2:3, :] * SPAN
    return base + meta[0:1, :] * 256.0 + meta[1:2, :], base


def score_kernel(tasks, sizes, columns_of, rows, last, *refs):
    block = rows + META
    refs = list(refs)
    arrays = [refs.pop(0) for _ in sizes]
    befores = [refs.pop(0) if more else None for _, _, more in tasks]
    place = refs.pop(0) if last else None
    columns = refs.pop()
    made = set()

    def column_of(name, index):
        if (name, index) not in made:
            made.add((name, index))
            line, _ = codes(arrays[name][index * block + rows : (index + 1) * block, :rows])
            columns[columns_of[name] + index] = jnp.broadcast_to(line, (128, rows)).T
        return columns[columns_of[name] + index]

    done = 0
    for number, (queries, keys, _) in enumerate(tasks):
        places = [(name, index) for name in queries for index in range(sizes[name])]
        for query, (query_name, query_index) in enumerate(places):
            at = query_index * block
            code, base = codes(arrays[query_name][at + rows : at + block, :rows])
            before = befores[number]
            most = jnp.full((8, rows), -1.0, jnp.float32) if before is None else before[query]
            for name in keys:
                for index in range(sizes[name]):
                    scores = lax.dot_general(
                        arrays[name][index * block : index * block + rows, :],
                        arrays[query_name][at : at + rows, :],
                        (((1,), (1,)), ((), ())),
                        preferred_element_type=jnp.float32,
                    )
                    column = column_of(name, index)
                    column = jnp.concatenate([column] * (rows // 128), axis=1)
                    allowed = (column < code) & (column >= base)
                    scores = jnp.where(allowed, scores, -1.0).reshape(rows // 8, 8, rows)
                    most = jnp.maximum(most, scores.max(axis=0))
            if last:
                refs[0][place[done]] = jnp.max(most, axis=0, keepdims=True)
            else:
                refs[number][query] = most
            done += 1


def score(tasks, rows, place=None):
    block = rows + META
    arrays = []

    def position(value):
        for index, other in enumerate(arrays):
            if other is value:
                return index
        arrays.append(value)
        return len(arrays) - 1

    plan = tuple(
        (tuple(map(position, queries)), tuple(map(position, keys)), before is not None)
        for queries, keys, before in tasks
    )
    width = arrays[0].shape[1]
    sizes = tuple(v.shape[0] // block for v in arrays)
    columns_of, count = {}, 0
    for _, keys, _ in plan:
        for name in keys:
            if name not in columns_of:
                columns_of[name] = count
                count += sizes[name]
    query_counts = [sum(sizes[n] for n in queries) for queries, _, _ in plan]
    pairs = sum(
        total * sum(sizes[n] for n in keys) for total, (_, keys, _) in zip(query_counts, plan)
    )
    befores = [before for _, _, before in tasks if before is not None]
    last = place is not None
    if last:
        out_shape = [jax.ShapeDtypeStruct((sum(query_counts), 1, rows), jnp.float32)]
    else:
        out_shape = [jax.ShapeDtypeStruct((total, 8, rows), jnp.float32) for total in query_counts]
    vmem = pl.BlockSpec(memory_space=pltpu.VMEM)
    return pl.pallas_call(
        functools.partial(score_kernel, plan, sizes, columns_of, rows, last),
        out_shape=out_shape,
        in_specs=[vmem] * (len(arrays) + len(befores))
        + [pl.BlockSpec(memory_space=pltpu.SMEM)] * last,
        out_specs=[vmem] * len(out_shape),
        scratch_shapes=[pltpu.VMEM((count, rows, 128), jnp.float32)],
        compiler_params=pltpu.CompilerParams(vmem_limit_bytes=4 * 1024 * 1024),
        cost_estimate=pl.CostEstimate(
            flops=2 * pairs * rows * width, bytes_accessed=10000, transcendentals=0
        ),
    )(*arrays, *befores, *([place] if last else []))


def pick_kernel(parts, block, *refs):
    out = refs[-1]
    for at, (name, index) in enumerate(parts):
        out[at * block : (at + 1) * block, :] = refs[name][index * block : (index + 1) * block, :]


def pick(parts, rows):
    block = rows + META
    arrays, plan = [], []
    for value, index in parts:
        known = [at for at, other in enumerate(arrays) if other is value]
        if not known:
            arrays.append(value)
        plan.append((known[0] if known else len(arrays) - 1, index))
    vmem = pl.BlockSpec(memory_space=pltpu.VMEM)
    return pl.pallas_call(
        functools.partial(pick_kernel, tuple(plan), block),
        out_shape=jax.ShapeDtypeStruct((len(parts) * block, arrays[0].shape[1]), arrays[0].dtype),
        in_specs=[vmem] * len(arrays),
        out_specs=vmem,
        compiler_params=pltpu.CompilerParams(vmem_limit_bytes=4 * 1024 * 1024),
        cost_estimate=pl.CostEstimate(flops=0, bytes_accessed=10000, transcendentals=0),
    )(*arrays)


def local(embeddings, owner, cluster, order):
    rows = embeddings.shape[0]
    index = lax.axis_index("grp")
    y, core = index // 2, index % 2
    side = 1 - 2 * core
    steps = jnp.stack([y, y, y + side, y + side, y - side, y - side, y + 2, y + 2]) % GRID
    types = jnp.stack([core, 1 - core, core, 1 - core, 1 - core, core, core, 1 - core])
    place = (steps * 2 + types).astype(jnp.int32)
    own, pair = prepare(embeddings, owner, cluster, order)
    pair, place = lax.optimization_barrier((pair, place))
    key_x = fetch(pair, 0, 1)
    key_z = fetch(pair, 2, 1)
    line_y = fetch(pair, 1, 1)
    key_xz = fetch(key_x, 2, -1)
    key_zx = fetch(pick([(key_x, 0), (key_z, 0), (key_z, 1)], rows), 0, 1)
    other_y = swap(line_y)
    line_y_later, other_y = lax.optimization_barrier((line_y, other_y))
    line_2y = fetch(line_y_later, 1, 1)
    front, back = [pair, line_y, other_y], [line_2y]
    near = [own, key_x, key_z]
    (best_front,) = score([(front, near, None)], rows)
    key_2z = fetch(pick([(key_z, 0)], rows), 2, 1)
    key_xz, best_front = lax.optimization_barrier((key_xz, best_front))
    key_2x2z = jump(key_2z, 0)
    key_xzz = fetch(key_xz, 2, -1)
    key_xxz = fetch(pick([(key_xz, 0)], rows), 0, 1)
    far = [key_xxz, key_xzz, fetch(pick([(key_zx, 0)], rows), 2, 1), key_2x2z]
    middle = [key_xz, key_zx, key_2z]
    best_front, best_back = score(
        [(front, middle, best_front), (back, near + middle, None)], rows
    )
    (best,) = score([(front, far, best_front), (back, far, best_back)], rows, place)
    home = lax.all_to_all(best, "grp", split_axis=0, concat_axis=0, tiled=True)
    return jnp.max(home.reshape(8, rows), axis=0)


def solution(mesh):
    placed = (
        P(("grp", "blk"), None),
        P(("grp", "blk"), None),
        P(("grp", "blk")),
        P(("grp", "blk")),
    )
    return jax.shard_map(
        local, mesh=mesh, in_specs=placed, out_specs=P(("grp", "blk")), check_vma=False
    )
```
